32 devices in a mesh: dp: 8 (over z, y), mp: 4 (over x, core).
Axes of the slice: x: 2, y: 2, z: 4, core: 2. Of those that a mesh axis runs over, the one named last changes fastest.
Arguments:
- inputs: bfloat16 [2, 8192, 1024], P(None, ('dp', 'mp')), may hold values from -6 to 6
- segments: int32 [2, 8192], P(None, 'dp'), may hold values from 0 to 3, as said below
- query_weight: bfloat16 [1024, 1024], P('dp', 'mp'), may hold values from -0.1875 to 0.1875
- key_weight: bfloat16 [1024, 1024], P('dp', 'mp'), may hold values from -0.1875 to 0.1875
- value_weight: bfloat16 [1024, 1024], P('dp', 'mp'), may hold values from -0.1875 to 0.1875
- out_weight: bfloat16 [1024, 1024], P('mp', 'dp'), may hold values from -3 to 3
- up_weight: bfloat16 [1024, 4096], P('dp', 'mp'), may hold values from -0.1875 to 0.1875
- down_weight: bfloat16 [4096, 1024], P('mp', 'dp'), may hold values from -0.09375 to 0.09375
- query_bias: float32 [1024], replicated, may hold values from -3 to 3
- value_bias: float32 [1024], replicated, may hold values from -0.3 to 0.3
- out_bias: float32 [1024], replicated, may hold values from -3 to 3
- up_bias: float32 [4096], replicated, may hold values from -3 to 3
- down_bias: float32 [1024], replicated, may hold values from -3 to 3
- first_gain: float32 [1024], replicated, may hold values from 0.25 to 1.75
- first_shift: float32 [1024], replicated, may hold values from -3 to 3
- second_gain: float32 [1024], replicated, may hold values from 0.25 to 1.75
- second_shift: float32 [1024], replicated, may hold values from -3 to 3
- cotangent: bfloat16 [2, 8192, 1024], P(None, ('dp', 'mp')), may hold values from -6 to 6
Outputs:
- outputs: bfloat16 [2, 8192, 1024], P(None, ('dp', 'mp'))
- input_grad: float32 [2, 8192, 1024], P(None, ('dp', 'mp'))
- grad_query: float32 [1024, 1024], P('dp', 'mp')
- grad_key: float32 [1024, 1024], P('dp', 'mp')
- grad_value: float32 [1024, 1024], P('dp', 'mp')
- grad_out: float32 [1024, 1024], P('mp', 'dp')
- grad_up: float32 [1024, 4096], P('dp', 'mp')
- grad_down: float32 [4096, 1024], P('mp', 'dp')
- grad_query_bias: float32 [1024], replicated
- grad_value_bias: float32 [1024], replicated
- grad_out_bias: float32 [1024], replicated
- grad_up_bias: float32 [4096], replicated
- grad_down_bias: float32 [1024], replicated
- grad_first_gain: float32 [1024], replicated
- grad_first_shift: float32 [1024], replicated
- grad_second_gain: float32 [1024], replicated
- grad_second_shift: float32 [1024], replicated
The draws below stay inside these ranges and needn't reach their ends.
Inputs may be any that keep to these rules, and one draw needn't show every extreme that they name: `segments`: within each aligned block of 1024 positions (one pack) the numbers never fall and all four of 0 to 3 occur; tokens attend only to tokens of their own pack with the same number.
All inputs are finite; a program needn't handle non-finite values.
Results may differ from the reference program's by a relative error of at most 0.018.
Values may be sent and summed in bfloat16 or wider, within the bound.
A program may use at most 192 MiB of HBM per device.

```python
import jax
import jax.numpy as jnp
from jax import lax

D = 1024
FF = 4096
HEADS = 16
HDIM = 64
PACK = 1024
MICRO = 2
BATCH_TOKENS = 8192
N_DP = 8
N_MP = 4


def draw_segments(key, part):
    key = jax.random.fold_in(key, 11)
    pack_count = MICRO * N_DP
    shard_rows = PACK // N_MP
    reach = max(shard_rows // 2, 2)
    key_start, key_inner, key_tail = jax.random.split(key, 3)
    start_long = jax.random.randint(key_start, (pack_count, 1), 2, reach + 2)
    inner_cut = jax.random.randint(key_inner, (pack_count, 1), 1, start_long)
    tail_len = jax.random.randint(key_tail, (pack_count, 1), 1, reach + 1)
    positions = jnp.arange(PACK, dtype=jnp.int32)[None, :]
    labels = (positions >= inner_cut).astype(jnp.int32) + (positions >= start_long).astype(jnp.int32) + (positions >= PACK - tail_len).astype(jnp.int32)
    return labels.reshape(MICRO, N_DP * PACK)


def level_of(own_key, extent, cuts, least, high):
    gain, own = 1.0, jax.random.fold_in(own_key, 6)
    for position, shards_of in cuts:
        draws = jnp.exp(jax.random.uniform(jax.random.fold_in(own, position), (shards_of,), jnp.float32, least / len(cuts), high / len(cuts)))
        gain = gain * jnp.repeat(draws, extent[position] // shards_of).reshape([-1 if axis == position else 1 for axis in range(len(extent))])
    return gain


def bell_draw(stream_key, extent, scale, limit, cuts=(), kind=jnp.bfloat16):
    factor_of = level_of(stream_key, extent, cuts, -0.22, 0.18) if cuts else 1.0
    drawn = jax.random.normal(stream_key, extent, jnp.float32) * scale * factor_of
    return jnp.minimum(jnp.maximum(drawn, -limit), limit).astype(kind)


def setup_inputs(seed: int = 0) -> dict:
    keys = jax.random.split(jax.random.key(seed), 19)
    return {
        "inputs": bell_draw(keys[0], (MICRO, BATCH_TOKENS, D), 1.0, 6.0, ((1, 32),)),
        "segments": draw_segments(jax.random.fold_in(keys[18], 71), 0),
        "query_weight": bell_draw(keys[2], (D, D), D ** -0.5, 0.1875, ((0, 8), (1, 4))),
        "key_weight": bell_draw(keys[3], (D, D), D ** -0.5, 0.1875, ((0, 8), (1, 4))),
        "value_weight": bell_draw(keys[4], (D, D), D ** -0.5, 0.1875, ((0, 8), (1, 4))),
        "out_weight": bell_draw(keys[5], (D, D), (max(D // 256, 1)) ** -0.5, 3.0, ((0, 4), (1, 8))),
        "up_weight": bell_draw(keys[6], (D, FF), D ** -0.5, 0.1875, ((0, 8), (1, 4))),
        "down_weight": bell_draw(keys[7], (FF, D), FF ** -0.5, 0.09375, ((0, 4), (1, 8))),
        "query_bias": bell_draw(keys[8], (D,), 0.5, 3.0, (), jnp.float32),
        "value_bias": bell_draw(keys[9], (D,), 0.05, 0.3, (), jnp.float32),
        "out_bias": bell_draw(keys[10], (D,), 0.5, 3.0, (), jnp.float32),
        "up_bias": bell_draw(keys[11], (FF,), 0.5, 3.0, (), jnp.float32),
        "down_bias": bell_draw(keys[12], (D,), 0.5, 3.0, (), jnp.float32),
        "first_gain": jnp.clip(1.0 + 0.15 * jax.random.normal(keys[13], (D,), jnp.float32), 0.25, 1.75),
        "first_shift": bell_draw(keys[14], (D,), 0.5, 3.0, (), jnp.float32),
        "second_gain": jnp.clip(1.0 + 0.15 * jax.random.normal(keys[15], (D,), jnp.float32), 0.25, 1.75),
        "second_shift": bell_draw(keys[16], (D,), 0.5, 3.0, (), jnp.float32),
        "cotangent": bell_draw(keys[17], (MICRO, BATCH_TOKENS, D), 1.0, 6.0, ((1, 32),)),
    }


@jax.custom_vjp
def low(v):
    return lax.optimization_barrier(v.astype(jnp.bfloat16)).astype(jnp.float32)

@jax.custom_vjp
def low_back(v):
    return v

def low_keep(v):
    return (low(v), None)

def low_pass(kept, grad):
    return (grad,)

def back_keep(v):
    return (v, None)

def back_low(kept, grad):
    return (low(grad),)
low.defvjp(low_keep, low_pass)
low_back.defvjp(back_keep, back_low)
epsilon = 1e-06
highest = lax.Precision.HIGHEST

def product(left_mat, right_mat):
    return jnp.dot(left_mat, right_mat, precision=highest, preferred_element_type=jnp.float32)

def layer_norm(residual, scale_vec, shift_vec):
    mean_val = lax.optimization_barrier(jnp.mean(residual, axis=-1, keepdims=True))
    centred = residual - mean_val
    variance = lax.optimization_barrier(jnp.mean(centred * centred, axis=-1, keepdims=True))
    return centred * lax.rsqrt(variance + epsilon) * scale_vec + shift_vec

def attend(pieces, key_heads, value_heads, key_segs):
    query_block, query_segs = pieces
    raw_scores = jnp.einsum('hqd,hkd->hqk', query_block, key_heads, precision=highest)
    same_doc = (query_segs[:, None] == key_segs[None, :])[None]
    scores = low_back(jnp.where(same_doc, raw_scores * HDIM ** (-0.5), -1000000000.0))
    top_val = lax.optimization_barrier(jnp.max(scores, axis=-1, keepdims=True))
    exponent = jnp.exp(scores - top_val)
    probabilities = low(exponent / lax.optimization_barrier(jnp.sum(exponent, axis=-1, keepdims=True)))
    return jnp.einsum('hqk,hkd->hqd', probabilities, value_heads, precision=highest)

def layer(tokens, seg_row, query_w, key_w, value_w, out_w, up_w, down_w, query_b, value_b, out_b, up_b, down_b, first_scale, first_offset, second_scale, second_offset):
    length = tokens.shape[0]
    block_rows = min(512, length)
    block_count = length // block_rows
    queries = low_back(low(product(tokens, query_w) + query_b))
    key_rows = low_back(low(product(tokens, key_w)))
    value_rows = low_back(low(product(tokens, value_w) + value_b))

    def head_major(matrix):
        return matrix.reshape(length, HEADS, HDIM).transpose(1, 0, 2)
    blocks = head_major(queries).reshape(HEADS, block_count, block_rows, HDIM).transpose(1, 0, 2, 3)
    key_heads = head_major(key_rows)
    value_heads = head_major(value_rows)
    context = lax.map(jax.checkpoint(lambda pieces: attend(pieces, key_heads, value_heads, seg_row)), (blocks, seg_row.reshape(block_count, block_rows)))
    context = context.transpose(0, 2, 1, 3).reshape(length, HEADS * HDIM)
    context = low_back(low(context))
    first_out = layer_norm(tokens + low_back(product(context, out_w)) + out_b, first_scale, first_offset)
    hidden = low_back(product(low(first_out), up_w) + up_b)
    active = low(jax.nn.gelu(hidden, approximate=False))
    return layer_norm(first_out + low_back(product(active, down_w)) + down_b, second_scale, second_offset)

def reference(inputs, segments, query_weight, key_weight, value_weight, out_weight, up_weight, down_weight, query_bias, value_bias, out_bias, up_bias, down_bias, first_gain, first_shift, second_gain, second_shift, cotangent):
    tokens = inputs.astype(jnp.float32).reshape(MICRO * N_DP, PACK, D)
    packed_segs = segments.reshape(MICRO * N_DP, PACK)
    params = tuple((tensor.astype(jnp.float32) for tensor in (query_weight, key_weight, value_weight, out_weight, up_weight, down_weight, query_bias, value_bias, out_bias, up_bias, down_bias, first_gain, first_shift, second_gain, second_shift)))

    def run_layer(token_packs, *weights):

        def one_pack(state_val, pack_item):
            return (state_val, jax.checkpoint(layer)(pack_item[0], pack_item[1], *weights))
        _, results = lax.scan(one_pack, jnp.float32(0.0), (token_packs, packed_segs))
        return results
    results, pull_back = jax.vjp(run_layer, tokens, *params)
    grads = pull_back(cotangent.astype(jnp.float32).reshape(MICRO * N_DP, PACK, D))
    outputs = results.reshape(MICRO, N_DP * PACK, D).astype(jnp.bfloat16)
    return (outputs, grads[0].reshape(MICRO, N_DP * PACK, D), grads[1], grads[2], grads[3], grads[4], grads[5], grads[6], grads[7], grads[8], grads[9], grads[10], grads[11], grads[12], grads[13], grads[14], grads[15])
```

```python
import functools

import jax
import jax.numpy as jnp
from jax import lax
from jax.sharding import PartitionSpec as P

HDIM = 64


epsilon = 1e-06


def matmul(left_mat, right_mat):
    return jnp.dot(left_mat, right_mat, preferred_element_type=jnp.float32)


def inner_rows(left_mat, right_mat):
    return lax.dot_general(
        left_mat, right_mat, (((0,), (0,)), ((), ())), preferred_element_type=jnp.float32
    )


def outer_cols(left_mat, right_mat):
    return lax.dot_general(
        left_mat, right_mat, (((1,), (1,)), ((), ())), preferred_element_type=jnp.float32
    )


def norm_forward(residual, scale_vec, shift_vec):
    mean_val = jnp.mean(residual, axis=-1, keepdims=True)
    centred = residual - mean_val
    inverse = lax.rsqrt(jnp.mean(centred * centred, axis=-1, keepdims=True) + epsilon)
    normed = centred * inverse
    return (normed * scale_vec + shift_vec, normed, inverse)


def norm_backward(incoming, normed, inverse, scale_vec):
    scaled = incoming * scale_vec
    centre_term = jnp.mean(scaled, axis=-1, keepdims=True)
    slope_term = jnp.mean(scaled * normed, axis=-1, keepdims=True)
    return (
        inverse * (scaled - centre_term - normed * slope_term),
        jnp.sum(incoming * normed, axis=0),
        jnp.sum(incoming, axis=0),
    )


def gelu_exact(values_in):
    return jax.nn.gelu(values_in, approximate=False)


def head_major(matrix, head_count):
    return matrix.reshape(matrix.shape[0], head_count, HDIM).transpose(1, 0, 2)


def head_blocks(matrix, head_count, block_rows):
    row_count = matrix.shape[0]
    return (
        head_major(matrix, head_count)
        .reshape(head_count, row_count // block_rows, block_rows, HDIM)
        .transpose(1, 0, 2, 3)
    )


def score_block(query_block, key_heads, query_segs, key_segs):
    raw_scores = jnp.einsum(
        "hqd,hkd->hqk", query_block, key_heads, preferred_element_type=jnp.float32
    )
    same_doc = (query_segs[:, None] == key_segs[None, :])[None]
    return jnp.where(same_doc, raw_scores * HDIM ** (-0.5), -1000000000.0)


def attention_forward(queries, key_rows, value_rows, seg_row, head_count):
    row_count = queries.shape[0]
    block_rows = min(512, row_count)
    key_heads = head_major(key_rows, head_count)
    value_heads = head_major(value_rows, head_count)

    def one_block(pieces):
        query_block, query_segs = pieces
        scores = score_block(query_block, key_heads, query_segs, seg_row)
        top_val = jnp.max(scores, axis=-1, keepdims=True)
        exponent = jnp.exp(scores - top_val)
        totals = jnp.sum(exponent, axis=-1, keepdims=True)
        probabilities = (exponent / totals).astype(jnp.bfloat16)
        context = jnp.einsum(
            "hqk,hkd->hqd", probabilities, value_heads, preferred_element_type=jnp.float32
        )
        return (context, (top_val + jnp.log(totals))[..., 0])

    context, log_totals = lax.map(
        one_block, (head_blocks(queries, head_count, block_rows), seg_row.reshape(-1, block_rows))
    )
    return (context.transpose(0, 2, 1, 3).reshape(row_count, head_count * HDIM), log_totals)


def attention_backward(
    queries, key_rows, value_rows, seg_row, log_totals, grad_context, head_count
):
    row_count = queries.shape[0]
    block_rows = min(512, row_count)
    key_heads = head_major(key_rows, head_count)
    value_heads = head_major(value_rows, head_count)
    scale_val = HDIM ** (-0.5)

    def one_block(sum_pair, pieces):
        query_block, grad_block, query_segs, block_lse = pieces
        scores = score_block(query_block, key_heads, query_segs, seg_row)
        probabilities = jnp.exp(scores - block_lse[..., None])
        grad_probs = jnp.einsum(
            "hqd,hkd->hqk", grad_block, value_heads, preferred_element_type=jnp.float32
        )
        grad_scores = (
            probabilities
            * (grad_probs - jnp.sum(grad_probs * probabilities, axis=-1, keepdims=True))
        ).astype(jnp.bfloat16)
        grad_query = (
            jnp.einsum("hqk,hkd->hqd", grad_scores, key_heads, preferred_element_type=jnp.float32)
            * scale_val
        )
        key_sum = (
            sum_pair[0]
            + jnp.einsum(
                "hqk,hqd->hkd", grad_scores, query_block, preferred_element_type=jnp.float32
            )
            * scale_val
        )
        value_sum = sum_pair[1] + jnp.einsum(
            "hqk,hqd->hkd",
            probabilities.astype(jnp.bfloat16),
            grad_block,
            preferred_element_type=jnp.float32,
        )
        return ((key_sum, value_sum), grad_query)

    zero_acc = jnp.zeros((head_count, row_count, HDIM), jnp.float32)
    pieces = (
        head_blocks(queries, head_count, block_rows),
        head_blocks(grad_context, head_count, block_rows),
        seg_row.reshape(-1, block_rows),
        log_totals,
    )
    (key_sum, value_sum), grad_query = lax.scan(one_block, (zero_acc, zero_acc), pieces)
    grad_query = grad_query.transpose(0, 2, 1, 3).reshape(row_count, head_count * HDIM)
    key_sum = key_sum.transpose(1, 0, 2).reshape(row_count, head_count * HDIM)
    value_sum = value_sum.transpose(1, 0, 2).reshape(row_count, head_count * HDIM)
    return (
        grad_query.astype(jnp.bfloat16),
        key_sum.astype(jnp.bfloat16),
        value_sum.astype(jnp.bfloat16),
    )


def steps_of(count):
    bit, found = count // 2, []
    while bit:
        found.append(bit)
        bit //= 2
    return found


def swap(block, axis_name, count, bit):
    return lax.ppermute(block, axis_name, [(i, i ^ bit) for i in range(count)])


def rank_order(count):
    order = [0]
    for bit in steps_of(count):
        order = order + [item ^ bit for item in order]
    return order


def gather_rows(block, count):
    for bit in steps_of(count):
        block = jnp.concatenate([block, swap(block, "mp", count, bit)], axis=0)
    return block


def scatter_rows(product_of, rows, count):
    half = rows // 2
    kept = None
    for bit in reversed(steps_of(count)):
        if kept is None:
            sent = product_of(half, rows).astype(jnp.bfloat16)
            came = swap(sent, "mp", count, bit)
            kept = product_of(0, half)
        else:
            sent = kept[half:].astype(jnp.bfloat16)
            came = swap(sent, "mp", count, bit)
            kept = kept[:half]
        kept = kept + came.astype(jnp.float32)
        half //= 2
    return kept


def gather_shards(block, count):
    rank = lax.axis_index("dp")
    rows = block.shape[0]
    width = block.shape[1]
    held = block.reshape(1, rows, width)
    for bit in steps_of(count):
        came = swap(held, "dp", count, bit)
        low = (rank & bit) == 0
        first = jnp.where(low, held, came)
        second = jnp.where(low, came, held)
        held = jnp.stack([first, second], axis=1).reshape(-1, rows, width)
    return held.reshape(count * rows, width)


def reduce_shards(total, count):
    rank = lax.axis_index("dp")
    rows = total.shape[0] // count
    held = total.reshape(count, rows, total.shape[1])
    for bit in reversed(steps_of(count)):
        pairs = held.reshape(held.shape[0] // 2, 2, rows, held.shape[2])
        low = (rank & bit) == 0
        sent = jnp.where(low, pairs[:, 1], pairs[:, 0])
        kept = jnp.where(low, pairs[:, 0], pairs[:, 1])
        came = swap(sent.astype(jnp.bfloat16), "dp", count, bit)
        held = kept.astype(jnp.float32) + came.astype(jnp.float32)
    return held[0]


def add_everywhere(vector, mp_count, dp_count):
    for axis_name, count in (("mp", mp_count), ("dp", dp_count)):
        for bit in steps_of(count):
            vector = vector + swap(vector, axis_name, count, bit)
    return vector


def gelu_pair(hidden):
    phi_cap = 0.5 * (1.0 + lax.erf(hidden * 0.7071067811865476))
    density = jnp.exp(-0.5 * hidden * hidden) * 0.3989422804014327
    return (
        (hidden * phi_cap).astype(jnp.bfloat16),
        (phi_cap + hidden * density).astype(jnp.bfloat16),
    )


def on_device(
    dp_count,
    mp_count,
    inputs,
    segments,
    query_weight,
    key_weight,
    value_weight,
    out_weight,
    up_weight,
    down_weight,
    query_bias,
    value_bias,
    out_bias,
    up_bias,
    down_bias,
    first_gain,
    first_shift,
    second_gain,
    second_shift,
    cotangent,
):
    micro_count = inputs.shape[0]
    head_cols = query_weight.shape[1]
    unit_cols = up_weight.shape[1]
    head_count = head_cols // HDIM
    mp_rank = lax.axis_index("mp")
    own_rows = inputs.shape[1]
    rows = own_rows * mp_count
    query_bias_own = lax.dynamic_slice_in_dim(query_bias, mp_rank * head_cols, head_cols)
    value_bias_own = lax.dynamic_slice_in_dim(value_bias, mp_rank * head_cols, head_cols)
    up_bias_own = lax.dynamic_slice_in_dim(up_bias, mp_rank * unit_cols, unit_cols)
    qkv_bias = jnp.concatenate([query_bias_own, jnp.zeros_like(query_bias_own), value_bias_own])
    order = [mp_rank ^ item for item in rank_order(mp_count)]

    qkv_all = gather_shards(
        jnp.concatenate([query_weight, key_weight, value_weight], axis=1), dp_count
    )
    out_t, up_all, down_t = (
        lax.all_gather(out_weight.T, "dp", axis=0, tiled=True),
        lax.all_gather(up_weight, "dp", axis=0, tiled=True),
        lax.all_gather(down_weight.T, "dp", axis=0, tiled=True),
    )

    results = []
    saved_list = []
    for micro in range(micro_count):
        own_tokens = inputs[micro]
        seg_blocks = segments[micro].reshape(mp_count, own_rows)
        seg_row = jnp.concatenate(
            [lax.dynamic_index_in_dim(seg_blocks, item, 0, keepdims=False) for item in order]
        )
        token_rows = gather_rows(own_tokens, mp_count)
        qkv = (matmul(token_rows, qkv_all) + qkv_bias).astype(jnp.bfloat16)
        queries = qkv[:, :head_cols]
        key_rows = qkv[:, head_cols : 2 * head_cols]
        value_rows = qkv[:, 2 * head_cols :]
        context, log_totals = attention_forward(queries, key_rows, value_rows, seg_row, head_count)
        context = context.astype(jnp.bfloat16)
        attention_out = scatter_rows(
            lambda low, high: outer_cols(context[low:high], out_t), rows, mp_count
        )
        first_out, first_normed, first_inverse = norm_forward(
            own_tokens.astype(jnp.float32) + attention_out + out_bias, first_gain, first_shift
        )
        first_rows = gather_rows(first_out.astype(jnp.bfloat16), mp_count)
        active, slope = lax.optimization_barrier(
            gelu_pair(matmul(first_rows, up_all) + up_bias_own)
        )
        feed_out = scatter_rows(
            lambda low, high: outer_cols(active[low:high], down_t), rows, mp_count
        )
        final_out, second_normed, second_inverse = norm_forward(
            first_out + feed_out + down_bias, second_gain, second_shift
        )
        results.append(final_out.astype(jnp.bfloat16))
        saved_list.append(
            (
                token_rows, seg_row, queries, key_rows, value_rows, log_totals, context,
                first_normed, first_inverse, first_rows, active, slope,
                second_normed, second_inverse,
            )
        )
    vector_sums = None
    input_grads = []
    pieces = []
    for micro in range(micro_count):
        (
            token_rows, seg_row, queries, key_rows, value_rows, log_totals, context,
            first_normed, first_inverse, first_rows, active, slope,
            second_normed, second_inverse,
        ) = saved_list[micro]
        incoming = cotangent[micro].astype(jnp.float32)
        grad_second, grad_second_gain, grad_second_shift = norm_backward(
            incoming, second_normed, second_inverse, second_gain
        )
        feed_rows = gather_rows(grad_second.astype(jnp.bfloat16), mp_count)
        grad_hidden = lax.optimization_barrier(
            (matmul(feed_rows, down_t) * slope.astype(jnp.float32)).astype(jnp.bfloat16)
        )
        grad_first = grad_second + scatter_rows(
            lambda low, high: outer_cols(grad_hidden[low:high], up_all), rows, mp_count
        )
        grad_resid, grad_first_gain, grad_first_shift = norm_backward(
            grad_first, first_normed, first_inverse, first_gain
        )
        attention_rows = gather_rows(grad_resid.astype(jnp.bfloat16), mp_count)
        grad_context = matmul(attention_rows, out_t).astype(jnp.bfloat16)
        grad_queries, grad_keys, grad_values = attention_backward(
            queries, key_rows, value_rows, seg_row, log_totals, grad_context, head_count
        )
        grad_qkv = jnp.concatenate([grad_queries, grad_keys, grad_values], axis=1)
        token_grad = scatter_rows(
            lambda low, high: outer_cols(grad_qkv[low:high], qkv_all), rows, mp_count
        )
        input_grads.append(grad_resid + token_grad)
        pieces.append(
            (token_rows, grad_qkv, attention_rows, context, first_rows, grad_hidden, feed_rows, active)
        )
        qkv_sums = jnp.sum(grad_qkv.astype(jnp.float32), axis=0)
        vector_terms = (
            qkv_sums[:head_cols],
            qkv_sums[2 * head_cols :],
            jnp.sum(grad_resid, axis=0),
            jnp.sum(grad_hidden.astype(jnp.float32), axis=0),
            jnp.sum(grad_second, axis=0),
            grad_first_gain,
            grad_first_shift,
            grad_second_gain,
            grad_second_shift,
        )
        vector_sums = (
            vector_terms
            if vector_sums is None
            else jax.tree.map(jnp.add, vector_sums, vector_terms)
        )

    def over_micros(left_place, right_place):
        total = inner_rows(pieces[0][left_place], pieces[0][right_place])
        for item in pieces[1:]:
            total = total + inner_rows(item[left_place], item[right_place])
        return total.astype(jnp.bfloat16)

    def scatter_sum(total):
        return lax.psum_scatter(total, "dp", scatter_dimension=0, tiled=True).astype(jnp.float32)

    ffn_sum = scatter_sum(jnp.concatenate([over_micros(6, 7), over_micros(4, 5)], axis=1))
    grad_down = ffn_sum[:, :unit_cols].T
    grad_up = ffn_sum[:, unit_cols:]
    att_sum = reduce_shards(jnp.concatenate([over_micros(0, 1), over_micros(2, 3)], axis=1), dp_count)
    grad_query = att_sum[:, :head_cols]
    grad_key = att_sum[:, head_cols : 2 * head_cols]
    grad_value = att_sum[:, 2 * head_cols : 3 * head_cols]
    grad_out = att_sum[:, 3 * head_cols :].T

    def widen(vector_part, full_size, offset):
        return lax.dynamic_update_slice_in_dim(
            jnp.zeros((full_size,), jnp.float32), vector_part, offset, 0
        )

    parts = (
        widen(vector_sums[0], query_bias.shape[0], mp_rank * head_cols),
        widen(vector_sums[1], value_bias.shape[0], mp_rank * head_cols),
        vector_sums[2],
        widen(vector_sums[3], up_bias.shape[0], mp_rank * unit_cols),
    ) + tuple(vector_sums[4:])
    joined = add_everywhere(
        jnp.concatenate(parts).reshape(-1, 128), mp_count, dp_count
    ).reshape(-1)
    summed, place = [], 0
    for part in parts:
        summed.append(joined[place : place + part.shape[0]])
        place += part.shape[0]
    return (
        jnp.stack(results),
        jnp.stack(input_grads),
        grad_query,
        grad_key,
        grad_value,
        grad_out,
        grad_up,
        grad_down,
    ) + tuple(summed)


def solution(mesh):
    in_specs = (
        P(None, ("dp", "mp"), None),
        P(None, "dp"),
        P("dp", "mp"),
        P("dp", "mp"),
        P("dp", "mp"),
        P("mp", "dp"),
        P("dp", "mp"),
        P("mp", "dp"),
        P(),
        P(),
        P(),
        P(),
        P(),
        P(),
        P(),
        P(),
        P(),
        P(None, ("dp", "mp"), None),
    )
    out_specs = (
        P(None, ("dp", "mp"), None),
        P(None, ("dp", "mp"), None),
        P("dp", "mp"),
        P("dp", "mp"),
        P("dp", "mp"),
        P("mp", "dp"),
        P("dp", "mp"),
        P("mp", "dp"),
        P(),
        P(),
        P(),
        P(),
        P(),
        P(),
        P(),
        P(),
        P(),
    )
    return jax.shard_map(
        functools.partial(on_device, mesh.shape["dp"], mesh.shape["mp"]), mesh=mesh, in_specs=in_specs, out_specs=out_specs, check_vma=False
    )
```

```python
import functools

import jax
import jax.numpy as jnp
from jax import lax
from jax.experimental import pallas as pl
from jax.experimental.pallas import tpu as pltpu
from jax.sharding import PartitionSpec as P

HDIM = 64


epsilon = 1e-06


def matmul(left_mat, right_mat):
    return jnp.dot(left_mat, right_mat, preferred_element_type=jnp.float32)


def inner_rows(left_mat, right_mat):
    return lax.dot_general(
        left_mat, right_mat, (((0,), (0,)), ((), ())), preferred_element_type=jnp.float32
    )


def outer_cols(left_mat, right_mat):
    return lax.dot_general(
        left_mat, right_mat, (((1,), (1,)), ((), ())), preferred_element_type=jnp.float32
    )


def norm_forward(residual, scale_vec, shift_vec):
    mean_val = jnp.mean(residual, axis=-1, keepdims=True)
    centred = residual - mean_val
    inverse = lax.rsqrt(jnp.mean(centred * centred, axis=-1, keepdims=True) + epsilon)
    normed = centred * inverse
    return (normed * scale_vec + shift_vec, normed, inverse)


def norm_backward(incoming, normed, inverse, scale_vec):
    scaled = incoming * scale_vec
    centre_term = jnp.mean(scaled, axis=-1, keepdims=True)
    slope_term = jnp.mean(scaled * normed, axis=-1, keepdims=True)
    return (
        inverse * (scaled - centre_term - normed * slope_term),
        jnp.sum(incoming * normed, axis=0),
        jnp.sum(incoming, axis=0),
    )


def gelu_exact(values_in):
    return jax.nn.gelu(values_in, approximate=False)


def head_lanes(matrix, index):
    lane = lax.broadcasted_iota(jnp.int32, matrix.shape, 1)
    return jnp.where(lane // HDIM == index, matrix, jnp.zeros_like(matrix))


def forward_kernel(query_ref, key_ref, value_ref, column_ref, row_ref, context_ref, lse_ref):
    rows, width = query_ref.shape
    block = min(256, rows)
    key_rows = key_ref[...]
    values = [head_lanes(value_ref[...], index) for index in range(width // HDIM)]
    key_segs = row_ref[...]

    def one_block(step, carry):
        span = pl.ds(pl.multiple_of(step * block, block), block)
        queries = query_ref[span, :] * jnp.asarray(HDIM ** (-0.5), jnp.bfloat16)
        same_doc = column_ref[span, :] == key_segs
        context = jnp.zeros((block, width), jnp.float32)
        for index in range(width // HDIM):
            scores = outer_cols(head_lanes(queries, index), key_rows)
            scores = jnp.where(same_doc, scores, -1000000000.0)
            top_val = jnp.max(scores, axis=-1, keepdims=True)
            exponent = jnp.exp(scores - top_val)
            total = jnp.sum(exponent, axis=-1, keepdims=True)
            context += matmul(exponent.astype(jnp.bfloat16), values[index]) / total
            lse_ref[0, span, index : index + 1] = top_val + jnp.log(total)
        context_ref[span, :] = context.astype(jnp.bfloat16)
        return carry

    lax.fori_loop(0, rows // block, one_block, 0)


def attention_forward(queries, key_rows, value_rows, seg_row):
    rows, head_cols = queries.shape
    width = min(128, head_cols)
    pairs = head_cols // width
    columns = pl.BlockSpec((rows, width), lambda pair: (0, pair))
    work = rows * rows * (head_cols // HDIM)
    return pl.pallas_call(
        forward_kernel,
        grid=(pairs,),
        in_specs=[
            columns,
            columns,
            columns,
            pl.BlockSpec((rows, 1), lambda pair: (0, 0)),
            pl.BlockSpec((1, rows), lambda pair: (0, 0)),
        ],
        out_specs=[columns, pl.BlockSpec((1, rows, width // HDIM), lambda pair: (pair, 0, 0))],
        out_shape=[
            jax.ShapeDtypeStruct((rows, head_cols), jnp.bfloat16),
            jax.ShapeDtypeStruct((pairs, rows, width // HDIM), jnp.float32),
        ],
        compiler_params=pltpu.CompilerParams(vmem_limit_bytes=32 * 1024 * 1024),
        cost_estimate=pl.CostEstimate(
            flops=4 * HDIM * work, bytes_accessed=8 * rows * head_cols, transcendentals=work
        ),
    )(queries, key_rows, value_rows, seg_row[:, None], seg_row[None, :])


def backward_kernel(
    query_ref, key_ref, value_ref, grad_ref, column_ref, row_ref, lse_ref,
    query_grad_ref, key_grad_ref, value_grad_ref, key_sum, value_sum,
):
    rows, width = query_ref.shape
    block = min(256, rows)
    key_rows, value_rows = key_ref[...], value_ref[...]
    keys = [head_lanes(key_rows, index) for index in range(width // HDIM)]
    key_segs = row_ref[...]
    key_sum[...] = jnp.zeros_like(key_sum)
    value_sum[...] = jnp.zeros_like(value_sum)

    def one_block(step, carry):
        span = pl.ds(pl.multiple_of(step * block, block), block)
        queries = query_ref[span, :] * jnp.asarray(HDIM ** (-0.5), jnp.bfloat16)
        grads = grad_ref[span, :]
        same_doc = column_ref[span, :] == key_segs
        query_grad = jnp.zeros((block, width), jnp.float32)
        for index in range(width // HDIM):
            query_head = head_lanes(queries, index)
            grad_head = head_lanes(grads, index)
            scores = outer_cols(query_head, key_rows)
            scores = jnp.where(same_doc, scores, -1000000000.0)
            probs = jnp.exp(scores - lse_ref[0, span, index : index + 1])
            grad_probs = outer_cols(grad_head, value_rows)
            slope = jnp.sum(grad_probs * probs, axis=-1, keepdims=True)
            grad_scores = (probs * (grad_probs - slope)).astype(jnp.bfloat16)
            query_grad += matmul(grad_scores, keys[index])
            key_sum[...] += inner_rows(grad_scores, query_head)
            value_sum[...] += inner_rows(probs.astype(jnp.bfloat16), grad_head)
        query_grad_ref[span, :] = (query_grad * HDIM ** (-0.5)).astype(jnp.bfloat16)
        return carry

    lax.fori_loop(0, rows // block, one_block, 0)
    key_grad_ref[...] = key_sum[...].astype(jnp.bfloat16)
    value_grad_ref[...] = value_sum[...].astype(jnp.bfloat16)


def attention_backward(queries, key_rows, value_rows, seg_row, lse, grad_context):
    rows, head_cols = queries.shape
    width = min(128, head_cols)
    pairs = head_cols // width
    columns = pl.BlockSpec((rows, width), lambda pair: (0, pair))
    work = rows * rows * (head_cols // HDIM)
    return pl.pallas_call(
        backward_kernel,
        grid=(pairs,),
        in_specs=[
            columns,
            columns,
            columns,
            columns,
            pl.BlockSpec((rows, 1), lambda pair: (0, 0)),
            pl.BlockSpec((1, rows), lambda pair: (0, 0)),
            pl.BlockSpec((1, rows, width // HDIM), lambda pair: (pair, 0, 0)),
        ],
        out_specs=[columns] * 3,
        out_shape=[jax.ShapeDtypeStruct((rows, head_cols), jnp.bfloat16)] * 3,
        scratch_shapes=[pltpu.VMEM((rows, width), jnp.float32)] * 2,
        compiler_params=pltpu.CompilerParams(vmem_limit_bytes=32 * 1024 * 1024),
        cost_estimate=pl.CostEstimate(
            flops=10 * HDIM * work, bytes_accessed=14 * rows * head_cols, transcendentals=work
        ),
    )(queries, key_rows, value_rows, grad_context, seg_row[:, None], seg_row[None, :], lse)


def steps_of(count):
    bit, found = count // 2, []
    while bit:
        found.append(bit)
        bit //= 2
    return found


def swap(block, axis_name, count, bit):
    return lax.ppermute(block, axis_name, [(i, i ^ bit) for i in range(count)])


def rank_order(count):
    order = [0]
    for bit in steps_of(count):
        order = order + [item ^ bit for item in order]
    return order


def gather_rows(block, count):
    for bit in steps_of(count):
        block = jnp.concatenate([block, swap(block, "mp", count, bit)], axis=0)
    return block


def scatter_rows(product_of, rows, count):
    half = rows // 2
    kept = None
    for bit in reversed(steps_of(count)):
        if kept is None:
            sent = product_of(half, rows).astype(jnp.bfloat16)
            came = swap(sent, "mp", count, bit)
            kept = product_of(0, half)
        else:
            sent = kept[half:].astype(jnp.bfloat16)
            came = swap(sent, "mp", count, bit)
            kept = kept[:half]
        kept = kept + came.astype(jnp.float32)
        half //= 2
    return kept, sent


def after(value, earlier):
    return value if earlier is None else lax.optimization_barrier((value, earlier))[0]


def gather_shards(block, count):
    rank = lax.axis_index("dp")
    rows = block.shape[0]
    width = block.shape[1]
    held = block.reshape(1, rows, width)
    for bit in steps_of(count):
        came = swap(held, "dp", count, bit)
        low = (rank & bit) == 0
        first = jnp.where(low, held, came)
        second = jnp.where(low, came, held)
        held = jnp.stack([first, second], axis=1).reshape(-1, rows, width)
    return held.reshape(count * rows, width)


def reduce_shards(total, count):
    rank = lax.axis_index("dp")
    rows = total.shape[0] // count
    held = total.reshape(count, rows, total.shape[1])
    for bit in reversed(steps_of(count)):
        pairs = held.reshape(held.shape[0] // 2, 2, rows, held.shape[2])
        low = (rank & bit) == 0
        sent = jnp.where(low, pairs[:, 1], pairs[:, 0])
        kept = jnp.where(low, pairs[:, 0], pairs[:, 1])
        came = swap(sent.astype(jnp.bfloat16), "dp", count, bit)
        held = kept.astype(jnp.float32) + came.astype(jnp.float32)
    return held[0]


def add_everywhere(vector, mp_count, dp_count):
    for axis_name, count in (("mp", mp_count), ("dp", dp_count)):
        for bit in steps_of(count):
            vector = vector + swap(vector, axis_name, count, bit)
    return vector


def gelu_pair(hidden):
    phi_cap = 0.5 * (1.0 + lax.erf(hidden * 0.7071067811865476))
    density = jnp.exp(-0.5 * hidden * hidden) * 0.3989422804014327
    return (
        (hidden * phi_cap).astype(jnp.bfloat16),
        (phi_cap + hidden * density).astype(jnp.bfloat16),
    )


def on_device(
    dp_count,
    mp_count,
    inputs,
    segments,
    query_weight,
    key_weight,
    value_weight,
    out_weight,
    up_weight,
    down_weight,
    query_bias,
    value_bias,
    out_bias,
    up_bias,
    down_bias,
    first_gain,
    first_shift,
    second_gain,
    second_shift,
    cotangent,
):
    micro_count = inputs.shape[0]
    head_cols = query_weight.shape[1]
    unit_cols = up_weight.shape[1]
    mp_rank = lax.axis_index("mp")
    own_rows = inputs.shape[1]
    rows = own_rows * mp_count
    query_bias_own = lax.dynamic_slice_in_dim(query_bias, mp_rank * head_cols, head_cols)
    value_bias_own = lax.dynamic_slice_in_dim(value_bias, mp_rank * head_cols, head_cols)
    up_bias_own = lax.dynamic_slice_in_dim(up_bias, mp_rank * unit_cols, unit_cols)
    qkv_bias = jnp.concatenate([query_bias_own, jnp.zeros_like(query_bias_own), value_bias_own])
    order = [mp_rank ^ item for item in rank_order(mp_count)]

    qkv_all = gather_shards(
        jnp.concatenate([query_weight, key_weight, value_weight], axis=1), dp_count
    )
    out_t = gather_shards(out_weight.T, dp_count)
    up_all, down_t = (
        lax.all_gather(up_weight, "dp", axis=0, tiled=True),
        lax.all_gather(down_weight.T, "dp", axis=0, tiled=True),
    )

    results = []
    saved_list = []
    heads_sent = units_sent = None
    for micro in range(micro_count):
        own_tokens = inputs[micro]
        seg_blocks = segments[micro].reshape(mp_count, own_rows)
        seg_row = jnp.concatenate(
            [lax.dynamic_index_in_dim(seg_blocks, item, 0, keepdims=False) for item in order]
        )
        token_rows = gather_rows(own_tokens, mp_count)
        qkv = (matmul(token_rows, qkv_all) + qkv_bias).astype(jnp.bfloat16)
        qkv = after(qkv, heads_sent)
        queries = qkv[:, :head_cols]
        key_rows = qkv[:, head_cols : 2 * head_cols]
        value_rows = qkv[:, 2 * head_cols :]
        context, log_totals = attention_forward(queries, key_rows, value_rows, seg_row)
        attention_out, heads_sent = scatter_rows(
            lambda low, high: outer_cols(context[low:high], out_t), rows, mp_count
        )
        first_out, first_normed, first_inverse = norm_forward(
            own_tokens.astype(jnp.float32) + attention_out + out_bias, first_gain, first_shift
        )
        first_rows = gather_rows(first_out.astype(jnp.bfloat16), mp_count)
        first_rows = after(first_rows, units_sent)
        active, slope = lax.optimization_barrier(
            gelu_pair(matmul(first_rows, up_all) + up_bias_own)
        )
        feed_out, units_sent = scatter_rows(
            lambda low, high: outer_cols(active[low:high], down_t), rows, mp_count
        )
        final_out, second_normed, second_inverse = norm_forward(
            first_out + feed_out + down_bias, second_gain, second_shift
        )
        results.append(final_out.astype(jnp.bfloat16))
        saved_list.append(
            (
                token_rows, seg_row, queries, key_rows, value_rows, log_totals, context,
                first_normed, first_inverse, first_rows, active, slope,
                second_normed, second_inverse,
            )
        )
    vector_sums = None
    input_grads = []
    pieces = []
    heads_sent = units_sent = None
    for micro in range(micro_count):
        (
            token_rows, seg_row, queries, key_rows, value_rows, log_totals, context,
            first_normed, first_inverse, first_rows, active, slope,
            second_normed, second_inverse,
        ) = saved_list[micro]
        incoming = cotangent[micro].astype(jnp.float32)
        grad_second, grad_second_gain, grad_second_shift = norm_backward(
            incoming, second_normed, second_inverse, second_gain
        )
        feed_rows = gather_rows(grad_second.astype(jnp.bfloat16), mp_count)
        feed_rows = after(feed_rows, units_sent)
        grad_hidden = lax.optimization_barrier(
            (matmul(feed_rows, down_t) * slope.astype(jnp.float32)).astype(jnp.bfloat16)
        )
        unit_terms, units_sent = scatter_rows(
            lambda low, high: outer_cols(grad_hidden[low:high], up_all), rows, mp_count
        )
        grad_first = grad_second + unit_terms
        grad_resid, grad_first_gain, grad_first_shift = norm_backward(
            grad_first, first_normed, first_inverse, first_gain
        )
        attention_rows = gather_rows(grad_resid.astype(jnp.bfloat16), mp_count)
        attention_rows = after(attention_rows, heads_sent)
        grad_context = matmul(attention_rows, out_t).astype(jnp.bfloat16)
        grad_queries, grad_keys, grad_values = attention_backward(
            queries, key_rows, value_rows, seg_row, log_totals, grad_context
        )
        grad_qkv = jnp.concatenate([grad_queries, grad_keys, grad_values], axis=1)
        token_grad, heads_sent = scatter_rows(
            lambda low, high: outer_cols(grad_qkv[low:high], qkv_all), rows, mp_count
        )
        input_grads.append(grad_resid + token_grad)
        pieces.append(
            (token_rows, grad_qkv, attention_rows, context, first_rows, grad_hidden, feed_rows, active)
        )
        qkv_sums = jnp.sum(grad_qkv.astype(jnp.float32), axis=0)
        vector_terms = (
            qkv_sums[:head_cols],
            qkv_sums[2 * head_cols :],
            jnp.sum(grad_resid, axis=0),
            jnp.sum(grad_hidden.astype(jnp.float32), axis=0),
            jnp.sum(grad_second, axis=0),
            grad_first_gain,
            grad_first_shift,
            grad_second_gain,
            grad_second_shift,
        )
        vector_sums = (
            vector_terms
            if vector_sums is None
            else jax.tree.map(jnp.add, vector_sums, vector_terms)
        )

    def over_micros(left_place, right_place):
        total = inner_rows(pieces[0][left_place], pieces[0][right_place])
        for item in pieces[1:]:
            total = total + inner_rows(item[left_place], item[right_place])
        return total.astype(jnp.bfloat16)

    def scatter_sum(total):
        return lax.psum_scatter(total, "dp", scatter_dimension=0, tiled=True).astype(jnp.float32)

    ffn_sum = scatter_sum(jnp.concatenate([over_micros(6, 7), over_micros(4, 5)], axis=1))
    grad_down = ffn_sum[:, :unit_cols].T
    grad_up = ffn_sum[:, unit_cols:]
    att_sum = reduce_shards(jnp.concatenate([over_micros(0, 1), over_micros(2, 3)], axis=1), dp_count)
    grad_query = att_sum[:, :head_cols]
    grad_key = att_sum[:, head_cols : 2 * head_cols]
    grad_value = att_sum[:, 2 * head_cols : 3 * head_cols]
    grad_out = att_sum[:, 3 * head_cols :].T

    def widen(vector_part, full_size, offset):
        return lax.dynamic_update_slice_in_dim(
            jnp.zeros((full_size,), jnp.float32), vector_part, offset, 0
        )

    parts = (
        widen(vector_sums[0], query_bias.shape[0], mp_rank * head_cols),
        widen(vector_sums[1], value_bias.shape[0], mp_rank * head_cols),
        vector_sums[2],
        widen(vector_sums[3], up_bias.shape[0], mp_rank * unit_cols),
    ) + tuple(vector_sums[4:])
    joined = add_everywhere(
        jnp.concatenate(parts).reshape(-1, 128), mp_count, dp_count
    ).reshape(-1)
    summed, place = [], 0
    for part in parts:
        summed.append(joined[place : place + part.shape[0]])
        place += part.shape[0]
    return (
        jnp.stack(results),
        jnp.stack(input_grads),
        grad_query,
        grad_key,
        grad_value,
        grad_out,
        grad_up,
        grad_down,
    ) + tuple(summed)


def solution(mesh):
    in_specs = (
        P(None, ("dp", "mp"), None),
        P(None, "dp"),
        P("dp", "mp"),
        P("dp", "mp"),
        P("dp", "mp"),
        P("mp", "dp"),
        P("dp", "mp"),
        P("mp", "dp"),
        P(),
        P(),
        P(),
        P(),
        P(),
        P(),
        P(),
        P(),
        P(),
        P(None, ("dp", "mp"), None),
    )
    out_specs = (
        P(None, ("dp", "mp"), None),
        P(None, ("dp", "mp"), None),
        P("dp", "mp"),
        P("dp", "mp"),
        P("dp", "mp"),
        P("mp", "dp"),
        P("dp", "mp"),
        P("mp", "dp"),
        P(),
        P(),
        P(),
        P(),
        P(),
        P(),
        P(),
        P(),
        P(),
    )
    return jax.shard_map(
        functools.partial(on_device, mesh.shape["dp"], mesh.shape["mp"]), mesh=mesh, in_specs=in_specs, out_specs=out_specs, check_vma=False
    )
```
